256 devices in a mesh: lat: 16 (over y_lo, x, core), lon: 16 (over y_hi, z).
Axes of the slice: x: 4, y: 4 (y_hi: 2, y_lo: 2; y = y_hi * 2 + y_lo), z: 8, core: 2. Of those that a mesh axis runs over, the one named last changes fastest.
Arguments:
- tokens: bfloat16 [4, 192, 384, 512], P(None, 'lat', 'lon'), may hold values from -6 to 6
- region_labels: int32 [4, 192, 384], P(None, 'lat', 'lon'), may hold values from 0 to 2
- fine_qkv: bfloat16 [512, 1536], replicated
- fine_proj: bfloat16 [512, 512], replicated, may hold values from -2 to 2
- merge_weight: bfloat16 [2048, 1024], replicated, may hold values from -0.125 to 0.125
- merged_qkv: bfloat16 [1024, 3072], P(None, 'lat')
- merged_proj: bfloat16 [1024, 1024], P('lat'), may hold values from -1.5 to 1.5
Outputs:
- fine_out: bfloat16 [4, 192, 384, 512], P(None, 'lat', 'lon')
- merged_out: bfloat16 [4, 96, 192, 1024], P(None, 'lat', 'lon')
The draws below stay inside these ranges and needn't reach their ends.
All inputs are finite; a program needn't handle non-finite values.
Results may differ from the reference program's by a relative error of at most 0.035.
Values may be sent and summed in bfloat16 or wider, within the bound.
A program may use at most 128 MiB of HBM per device.

```python
import math
import jax
import jax.numpy as jnp
from jax import lax

D1 = 512
HEADS1 = 8
D2 = 1024
HEADS2 = 16
WLAT = 6
WLON = 12
LEV = 4
NLAT = 192
NLON = 384


def draw_projection(key, rows_in, head_count, head_size, low_scale, high_scale):
    first, second = jax.random.split(key)
    base = jax.random.normal(first, (rows_in, head_count, 3, head_size), jnp.float32) * rows_in ** (-0.5)
    scales = jnp.exp(jax.random.uniform(second, (head_count,), jnp.float32, math.log(low_scale), math.log(high_scale)))
    queries = base[:, :, 0] * scales[None, :, None]
    paired = base[:, :, 1]
    paired = paired * scales[None, :, None]
    return jnp.stack([queries, paired, base[:, :, 2]], axis=2)


def draw_tokens(key, part):
    key = jax.random.fold_in(key, 1)
    first = jax.random.fold_in(key, 0)
    shape = (LEV, NLAT, NLON, D1)
    values = jax.random.normal(first, shape, jnp.float32)
    return jnp.clip(values, -6.0, 6.0).astype(jnp.bfloat16)


def draw_fine_qkv(key, part):
    key = jax.random.fold_in(key, 2)
    low_scale, high_scale = (1.0, 1.0)
    columns = draw_projection(key, D1, HEADS1, D1 // HEADS1, low_scale, high_scale)
    return columns.transpose(0, 2, 1, 3).reshape(D1, 3 * D1).astype(jnp.bfloat16)


def draw_merged_qkv(key, part):
    key = jax.random.fold_in(key, 3)
    low_scale, high_scale = (1.0, 1.0)
    columns = draw_projection(key, D2, HEADS2, D2 // HEADS2, low_scale, high_scale)
    return columns.reshape(D2, 3 * D2).astype(jnp.bfloat16)


def place_ends(values, key, low, top_value):
    dims = values.shape
    index_at = [jax.random.randint(jax.random.fold_in(key, axis), (), 0, dims[axis]) for axis in range(len(dims))]
    values = values.at[tuple(index_at)].set(low)
    longest = dims.index(max(dims))
    index_at[longest] = (index_at[longest] + 1) % dims[longest]
    return values.at[tuple(index_at)].set(top_value)


def level_of(rng, dims, pieces, smallest, high):
    def one(position, shards_of):
        heights = jax.random.uniform(jax.random.fold_in(jax.random.fold_in(rng, 6), position), (shards_of,), jnp.float32, smallest / len(pieces), high / len(pieces))
        return jnp.repeat(jnp.exp(heights), dims[position] // shards_of).reshape((-1,) + (1,) * (len(dims) - position - 1))

    level = one(*pieces[0])
    for cut in pieces[1:]:
        level = level * one(*cut)
    return level


def bell_draw(stream_key, shape, scale, reach, cuts=(), kind=jnp.bfloat16):
    values = jax.random.normal(stream_key, shape, jnp.float32) * scale
    if len(cuts) > 0:
        values = level_of(stream_key, shape, cuts, -0.22, 0.18) * values
    return jnp.clip(values, min=-reach, max=reach).astype(kind)


def setup_inputs(seed: int = 0) -> dict:
    seeds = jax.random.split(jax.random.key(seed), 8)
    tokens = draw_tokens(jax.random.fold_in(seeds[7], 71), 0)
    region_labels = place_ends(jax.random.randint(seeds[1], (LEV, NLAT, NLON), 0, 3), jax.random.fold_in(seeds[1], 1), 0, 2).astype(jnp.int32)
    fine_qkv = draw_fine_qkv(jax.random.fold_in(seeds[7], 71), 0)
    fine_proj = bell_draw(seeds[3], (D1, D1), (max(D1 // 64, 1)) ** -0.5, 2.0)
    merge_weight = bell_draw(seeds[4], (4 * D1, D2), (4 * D1) ** -0.5, 0.125)
    merged_qkv = draw_merged_qkv(jax.random.fold_in(seeds[7], 71), 0)
    merged_proj = bell_draw(seeds[6], (D2, D2), (max(D2 // 64, 1)) ** -0.5, 1.5, ((0, 16),))
    return dict(tokens=tokens, region_labels=region_labels, fine_qkv=fine_qkv, fine_proj=fine_proj, merge_weight=merge_weight, merged_qkv=merged_qkv, merged_proj=merged_proj)


epsilon = 1e-05
masked_score = -1e+30

def layer_norm(values):
    average = lax.optimization_barrier(jnp.mean(values, axis=-1, keepdims=True))
    centred = values - average
    spread = lax.optimization_barrier(jnp.mean(centred * centred, axis=-1, keepdims=True))
    return centred * lax.rsqrt(spread + epsilon)

def to_windows(grid, win_rows, win_cols):
    levels, rows_all, cols_all, features = grid.shape
    blocks = grid.reshape(levels, rows_all // win_rows, win_rows, cols_all // win_cols, win_cols, features)
    blocks = blocks.transpose(1, 3, 0, 2, 4, 5)
    return blocks.reshape(rows_all // win_rows, cols_all // win_cols, levels * win_rows * win_cols, features)

def from_windows(blocks, levels, win_rows, win_cols):
    row_windows, col_windows, length, features = blocks.shape
    grid = blocks.reshape(row_windows, col_windows, levels, win_rows, win_cols, features)
    grid = grid.transpose(2, 0, 3, 1, 4, 5)
    return grid.reshape(levels, row_windows * win_rows, col_windows * win_cols, features)

def attend(query_rows, key_rows, value_rows, head_count, allowed):
    windows, length, model_width = query_rows.shape
    head_size = model_width // head_count
    query_heads = query_rows.reshape(windows, length, head_count, head_size).astype(jnp.float32)
    key_heads = key_rows.reshape(windows, length, head_count, head_size).astype(jnp.float32)
    value_heads = value_rows.reshape(windows, length, head_count, head_size).astype(jnp.float32)
    scores = jnp.einsum('wqhd,wkhd->whqk', query_heads, key_heads) * (1.0 / math.sqrt(head_size))
    if allowed is not None:
        scores = jnp.where(allowed[:, None, :, :], scores, masked_score)
    scores = scores - lax.optimization_barrier(jnp.max(scores, axis=-1, keepdims=True))
    expd = jnp.exp(scores)
    soft_weights = (expd / lax.optimization_barrier(jnp.sum(expd, axis=-1, keepdims=True))).astype(jnp.bfloat16)
    mixture = jnp.einsum('whqk,wkhd->wqhd', soft_weights.astype(jnp.float32), value_heads)
    return mixture.astype(jnp.bfloat16).reshape(windows, length, model_width)

def merge_patches(fine_grid, merge_weight):
    levels, rows_all, cols_all, features = fine_grid.shape
    blocks = fine_grid.reshape(levels, rows_all // 2, 2, cols_all // 2, 2, features)
    blocks = blocks.transpose(0, 1, 3, 4, 2, 5).reshape(levels, rows_all // 2, cols_all // 2, 4 * features)
    normed_cat = layer_norm(blocks.astype(jnp.float32)).astype(jnp.bfloat16)
    merged = jnp.dot(normed_cat.reshape(-1, 4 * features), merge_weight, preferred_element_type=jnp.float32)
    return merged.astype(jnp.bfloat16).reshape(levels, rows_all // 2, cols_all // 2, merge_weight.shape[1])

def coarse_block(merged_in, merged_qkv, merged_proj):
    levels, coarse_rows, coarse_cols, model_width = merged_in.shape
    head_size = model_width // HEADS2
    normed = layer_norm(merged_in.astype(jnp.float32)).astype(jnp.bfloat16)
    acts = jnp.dot(normed.reshape(-1, model_width), merged_qkv, preferred_element_type=jnp.float32)
    acts = acts.astype(jnp.bfloat16).reshape(levels, coarse_rows, coarse_cols, 3 * model_width)
    grouped = to_windows(acts, WLAT, WLON)

    def one_row(window_row):
        col_windows = window_row.shape[0]
        length = window_row.shape[1]
        split = window_row.reshape(col_windows, length, HEADS2, 3, head_size)
        return attend(split[:, :, :, 0].reshape(col_windows, length, model_width), split[:, :, :, 1].reshape(col_windows, length, model_width), split[:, :, :, 2].reshape(col_windows, length, model_width), HEADS2, None)
    result = from_windows(lax.map(one_row, grouped), levels, WLAT, WLON)
    update = jnp.dot(result.reshape(-1, model_width), merged_proj, preferred_element_type=jnp.float32)
    total = merged_in.reshape(-1, model_width).astype(jnp.float32) + update
    return total.astype(jnp.bfloat16).reshape(merged_in.shape)

def reference(tokens, region_labels, fine_qkv, fine_proj, merge_weight, merged_qkv, merged_proj):
    lat_shift = WLAT // 2
    lon_shift = WLON // 2
    normed = layer_norm(tokens.astype(jnp.float32)).astype(jnp.bfloat16)
    acts = jnp.dot(normed.reshape(-1, D1), fine_qkv, preferred_element_type=jnp.float32)
    acts = acts.astype(jnp.bfloat16).reshape(LEV, NLAT, NLON, 3 * D1)
    rolled_acts = jnp.roll(acts, (-lat_shift, -lon_shift), axis=(1, 2))
    rolled_labels = jnp.roll(region_labels, (-lat_shift, -lon_shift), axis=(1, 2))
    seam = (jnp.arange(NLAT) >= NLAT - lat_shift).astype(jnp.int32)
    window_key = rolled_labels * 4 + seam[None, :, None]
    grouped = to_windows(rolled_acts, WLAT, WLON)
    grouped_keys = to_windows(window_key[..., None], WLAT, WLON)[..., 0]

    def one_row(pair):
        window_row, key_row = pair
        allowed = key_row[:, :, None] == key_row[:, None, :]
        return attend(window_row[..., :D1], window_row[..., D1:2 * D1], window_row[..., 2 * D1:], HEADS1, allowed)
    attn_rolled = from_windows(lax.map(one_row, (grouped, grouped_keys)), LEV, WLAT, WLON)
    fine_attn = jnp.roll(attn_rolled, (lat_shift, lon_shift), axis=(1, 2))
    update = jnp.dot(fine_attn.reshape(-1, D1), fine_proj, preferred_element_type=jnp.float32).astype(jnp.bfloat16)
    fine_out = (tokens.astype(jnp.float32) + update.reshape(tokens.shape).astype(jnp.float32)).astype(jnp.bfloat16)
    merged_in = merge_patches(fine_out, merge_weight)
    merged_out = coarse_block(merged_in, merged_qkv, merged_proj)
    return (fine_out, merged_out)
```

```python
import functools
import math

import jax
import jax.numpy as jnp
import numpy as np
from jax import lax
from jax.experimental import pallas as pl
from jax.experimental.pallas import tpu as pltpu
from jax.sharding import PartitionSpec as P

MESH = pl.DeviceIdType.MESH
BF = jnp.bfloat16
F32 = jnp.float32

D1 = 512
D2 = 1024
EPS = 1e-05
BIG = 1e32
COEF = 0.125 * math.log2(math.e)

ROWS = 464
LO = (0, 160, 304)
HI = (160, 304, 464)
QLO = (80, 160, 304)
QHI = (160, 304, 384)
BLOCKS = ((0, 72), (80, 72), (160, 72), (232, 72), (304, 72), (384, 72))

OWN, LEFT, RIGHT, OTHER, OLEFT, ORIGHT, FAR, OFAR = range(8)


def constants():
    order = np.zeros((304, 288), np.float32)
    rowsel = np.zeros((4, ROWS, 64), np.float32)
    colsel = np.zeros((ROWS, 384), np.float32)
    rowsel[:, :, 12] = 1.0
    colsel[:, 0] = 1.0
    for block, (start, _) in enumerate(BLOCKS):
        for lev in range(4):
            for r in range(3):
                for c in range(6):
                    at = start + lev * 18 + r * 6 + c
                    if 1 <= block <= 4:
                        order[at - 80, lev * 72 + r * 24 + (block - 1) * 6 + c] = 1.0
                    tile, col = ((0, 18 + c), (1, c), (1, 6 + c), (1, 12 + c), (1, 18 + c), (2, c))[block]
                    colsel[at] = 0.0
                    colsel[at, tile * 128 + col] = 1.0
                    for a in range(4):
                        rowsel[a, at] = 0.0
                        rowsel[a, at, lev * 16 + 3 * a + r] = 1.0
    sel = np.zeros((288, 288), np.float32)
    for s in range(4):
        for r in range(6):
            for c in range(12):
                sel[s * 72 + r * 12 + c, (2 * r + s % 2) * 24 + 2 * c + s // 2] = 1.0
    cast = lambda v: jnp.asarray(v, BF)
    return cast(order), cast(order.T.copy()), cast(sel), cast(rowsel), cast(colsel)


def nt(a, b):
    return lax.dot_general(a, b, (((1,), (1,)), ((), ())), preferred_element_type=F32)


def nn(a, b):
    return jnp.dot(a, b, preferred_element_type=F32)


def norm(v):
    v = v - jnp.mean(v, axis=-1, keepdims=True)
    return v * lax.rsqrt(jnp.mean(v * v, axis=-1, keepdims=True) + EPS)


def pair_attention(q, kx, vx, aug):
    n = q.shape[0]
    even = lax.broadcasted_iota(jnp.int32, (n, 128), 1) < 64
    zero = jnp.zeros_like(q)
    heads = jnp.concatenate([jnp.where(even, q, zero), jnp.where(even, zero, q)], axis=0)
    if aug is not None:
        heads = jnp.concatenate([heads, jnp.concatenate([aug, aug], axis=0)], axis=1)
    s = nt(heads, kx)
    e = jnp.exp2((s - jnp.max(s, axis=-1, keepdims=True)) * COEF).astype(BF)
    o = nn(e, vx)
    return jnp.where(even, o[:n, :128] / o[:n, 128:], o[n:, :128] / o[n:, 128:]).astype(BF)


def kernel(
    nlat, nlon,
    tok, lab, wqkv_h, wproj_h, wmerge_h, mqkv_h, mproj_h, order_h, back_h, sel_h, rowsel_h, colsel_h,
    fine_out, merged_out,
    x, lx, wqkv, wproj, wmerge, mqkv, order, back, sel, rowsel, colsel,
    ext, aug, lf, qs, kx, vx, at, fo, mn, g, cq, ca, mo,
    load_sem, lab_send, lab_recv, halo_send, halo_recv, w_send, w_recv, out_sem,
):
    i, j = lax.axis_index("lat"), lax.axis_index("lon")
    up, down = (i + nlat - 1) % nlat, (i + 1) % nlat
    west, east = (j + nlon - 1) % nlon, (j + 1) % nlon
    core = i % 2
    chip = (i // 2) % 4
    ylo = i // 8
    partner = i + 1 - 2 * core
    xl = ylo * 8 + ((chip + 3) % 4) * 2 + core
    xr = ylo * 8 + ((chip + 1) % 4) * 2 + core
    yo = (i + 8) % nlat
    jo = (j + 8) % nlon

    around = [(up, j), (down, j), (i, west), (i, east), (up, west), (up, east), (down, west), (down, east)]
    opposite = [1, 0, 3, 2, 7, 6, 5, 4]
    barrier = pltpu.get_barrier_semaphore()
    others = around + [(xl, j), (xr, j), (yo, j), (yo, jo)]
    for other in others:
        pl.semaphore_signal(barrier, inc=1, device_id=other, device_id_type=MESH)

    loads = [
        pltpu.make_async_copy(src, dst, load_sem.at[n])
        for n, (src, dst) in enumerate([
            (tok, x), (lab, lx.at[1, 1]), (order_h, order), (mqkv_h, mqkv), (mproj_h, g.at[OWN, 0, pl.ds(192, 64)]),
            (rowsel_h, rowsel), (colsel_h, colsel), (wqkv_h, wqkv), (back_h, back), (sel_h, sel), (wproj_h, wproj),
            (wmerge_h, wmerge),
        ])
    ]
    for copy in loads:
        copy.start()
    (l_tok, l_lab, l_order, l_mqkv, l_mproj, l_rowsel, l_colsel, l_wqkv, l_back, l_sel, l_wproj, l_wmerge) = loads

    def remote(src, dst, send, recv, device):
        return pltpu.make_async_remote_copy(
            src_ref=src, dst_ref=dst, send_sem=send, recv_sem=recv, device_id=device, device_id_type=MESH
        )

    l_tok.wait()
    l_order.wait()

    def prepare(a, carry):
        rows = x[:, a].reshape(288, D1).astype(F32)
        ext[a + 1, 80:384] = nn(order[...], norm(rows).astype(BF)).astype(BF)
        return carry

    lax.fori_loop(0, 4, prepare, 0)
    l_mqkv.wait()
    eye = lax.broadcasted_iota(jnp.int32, (192, 192), 0) == lax.broadcasted_iota(jnp.int32, (192, 192), 1)
    g[OWN, 0, 0:192] = nt(eye.astype(F32).astype(BF), mqkv[...]).astype(BF)
    l_mproj.wait()
    l_lab.wait()

    pl.semaphore_wait(barrier, len(others))
    places = [(2, 1), (0, 1), (1, 2), (1, 0), (2, 2), (2, 0), (0, 2), (0, 0)]
    lab_copies = [
        remote(lx.at[1, 1], lx.at[places[n][0], places[n][1]], lab_send.at[n], lab_recv.at[n], around[n]) for n in range(8)
    ]
    own, first, last = pl.ds(80, 304), pl.ds(80, 80), pl.ds(304, 80)
    to_east, to_west = pl.ds(384, 80), pl.ds(0, 80)
    inner = pl.ds(1, 4)
    halo = [
        (ext.at[1, own], ext.at[5, own]),
        (ext.at[4, own], ext.at[0, own]),
        (ext.at[inner, first], ext.at[inner, to_east]),
        (ext.at[inner, last], ext.at[inner, to_west]),
        (ext.at[1, first], ext.at[5, to_east]),
        (ext.at[1, last], ext.at[5, to_west]),
        (ext.at[4, first], ext.at[0, to_east]),
        (ext.at[4, last], ext.at[0, to_west]),
    ]
    halo_copies = [remote(src, dst, halo_send.at[n], halo_recv.at[n], around[n]) for n, (src, dst) in enumerate(halo)]
    for n in (2, 3, 0, 1, 4, 5, 6, 7):
        halo_copies[n].start()
        lab_copies[n].start()

    lower, upper = pl.ds(0, 128), pl.ds(128, 128)
    w_list = []

    def weights(src, dst, device):
        n = len(w_list)
        w_list.append(remote(src, dst, w_send.at[n], w_recv.at[n], device))
        return w_list[-1]

    def across(src, dst):
        a = weights(g.at[src, 0, lower], g.at[dst, 0, lower], (yo, j))
        b = weights(g.at[src, 0, upper], g.at[dst, 0, upper], (yo, jo))
        return [a, b]

    def share(slot):
        return [weights(g.at[slot, 0], g.at[slot, 1], (partner, j))]

    own_right = weights(g.at[OWN, 0], g.at[LEFT, 0], (xr, j))
    own_left = weights(g.at[OWN, 0], g.at[RIGHT, 0], (xl, j))
    own_across = across(OWN, OTHER)
    own_share = share(OWN)
    far_right = weights(g.at[LEFT, 0, lower], g.at[FAR, 0, lower], (xr, j))
    far_left = weights(g.at[RIGHT, 0, upper], g.at[FAR, 0, upper], (xl, j))
    left_across = across(LEFT, OLEFT)
    right_across = across(RIGHT, ORIGHT)
    far_across = across(FAR, OFAR)
    left_share, right_share, other_share = share(LEFT), share(RIGHT), share(OTHER)
    oleft_share, oright_share, far_share, ofar_share = share(OLEFT), share(ORIGHT), share(FAR), share(OFAR)

    def start(*groups):
        for group in groups:
            for copy in group:
                copy.start()

    def arrived(*groups):
        for group in groups:
            for copy in group:
                copy.wait_recv()

    start([own_right, own_left], own_across, own_share)

    def window_keys(a, a_rows, t_lat, seam):
        codes = nn(rowsel[a_rows], lf[t_lat].astype(BF)) * colsel[...].astype(F32)
        codes = nn(codes.astype(BF), jnp.ones((384, 128), BF)) + seam
        lanes = lax.broadcasted_iota(jnp.int32, (ROWS, 128), 1).astype(F32)
        aug[a] = jnp.where(codes == lanes, 1.0, 0.0).astype(BF)

    lf[...] = jnp.full(lf.shape, 7.0, F32)

    def labels_of(t_lat, t_lon):
        for lev in range(4):
            lf[t_lat, lev * 16 : lev * 16 + 12, t_lon * 128 : t_lon * 128 + 24] = lx[t_lat, t_lon, lev].astype(F32)

    vx[:, :, 128:256] = jnp.ones((4, 320, 128), BF)
    l_rowsel.wait()
    l_colsel.wait()
    l_wqkv.wait()
    for copy in lab_copies:
        copy.wait_recv()
    for t_lat in range(3):
        for t_lon in range(3):
            labels_of(t_lat, t_lon)
    first_row = jnp.where(i == 0, 3.0, 0.0)
    last_row = jnp.where(i == nlat - 1, 3.0, 0.0)
    for a, (a_rows, t_lat, seam) in enumerate(
        [(3, 0, 0.0), (0, 1, first_row), (1, 1, 0.0), (2, 1, 0.0), (3, 1, 0.0), (0, 2, last_row)]
    ):
        window_keys(a, a_rows, t_lat, seam)

    def window(u, v):
        lo, hi = LO[v], HI[v]
        count = 2 * (hi - lo)
        rows = jnp.concatenate([ext[2 * u, lo:hi], ext[2 * u + 1, lo:hi]], axis=0)
        keys = nn(rows, wqkv[:, D1 : 2 * D1]).astype(BF)
        values = nn(rows, wqkv[:, 2 * D1 :]).astype(BF)
        marks = jnp.concatenate([aug[2 * u, lo:hi], aug[2 * u + 1, lo:hi]], axis=0)
        for p in range(4):
            kx[p, 0:count, 0:128] = keys[:, p * 128 : (p + 1) * 128]
            kx[p, 0:count, 128:256] = marks
            vx[p, 0:count, 0:128] = values[:, p * 128 : (p + 1) * 128]
        mine = ((1,), (2, 3), (4,))[u]
        qlo, qhi = QLO[v], QHI[v]
        each = qhi - qlo
        q = nn(jnp.concatenate([ext[a, qlo:qhi] for a in mine], axis=0), wqkv[:, 0:D1]).astype(BF)
        q_marks = jnp.concatenate([aug[a, qlo:qhi] for a in mine], axis=0)
        q_marks = ((q_marks.astype(F32) - 1.0) * BIG).astype(BF)
        total = each * len(mine)
        for p in range(4):
            qs[p, 0:total] = q[:, p * 128 : (p + 1) * 128]

        def pair(p, carry):
            out = pair_attention(qs[p, 0:total], kx[p, 0:count], vx[p, 0:count], q_marks)
            for n, a in enumerate(mine):
                at[p, a - 1, qlo - 80 : qhi - 80] = out[n * each : (n + 1) * each]
            return carry

        lax.fori_loop(0, 4, pair, 0)

    window(1, 1)
    arrived([halo_copies[0], halo_copies[1]])
    window(0, 1)
    window(2, 1)
    arrived([halo_copies[2], halo_copies[3]])
    window(1, 0)
    window(1, 2)
    arrived([own_right, own_left], own_across)
    start([far_right, far_left], left_across, right_across, left_share, right_share, other_share)
    arrived(halo_copies[4:8])
    window(0, 0)
    window(0, 2)
    window(2, 0)
    window(2, 2)

    l_back.wait()
    l_wproj.wait()

    def finish(a, carry):
        heads = jnp.concatenate([at[p, a] for p in range(4)], axis=1)
        update = nn(heads, wproj[...]).astype(BF)
        natural = nn(back[...], update).reshape(4, 72, D1)
        fo[:, a] = (x[:, a].astype(F32) + natural).astype(BF)
        return carry

    lax.fori_loop(0, 4, finish, 0)
    out_fine = pltpu.make_async_copy(fo, fine_out, out_sem.at[0])
    out_fine.start()
    arrived([far_right, far_left])
    start(far_across, far_share)

    l_sel.wait()

    def merge(lev, carry):
        parts = nn(sel[...], fo[lev].reshape(288, D1))
        cat = jnp.concatenate([parts[s * 72 : (s + 1) * 72] for s in range(4)], axis=1)
        mn[lev] = norm(cat)
        return carry

    lax.fori_loop(0, 4, merge, 0)
    l_wmerge.wait()
    merged_in = nn(mn[...].reshape(288, 4 * D1).astype(BF), wmerge[...]).astype(BF)
    mo[...] = merged_in
    normed = norm(merged_in.astype(F32)).astype(BF)
    arrived(left_across, right_across)
    start(oleft_share, oright_share)

    def coarse(slot):
        take = lambda lo: g[slot : slot + 2, :, lo : lo + 64].reshape(256, D2)
        q = nt(normed, take(0)).astype(BF)
        k = nt(normed, take(64)).astype(BF)
        v = nt(normed, take(128)).astype(BF)
        for p in range(2):
            cq[p, 0] = q[:, p * 128 : (p + 1) * 128]
            cq[p, 1] = k[:, p * 128 : (p + 1) * 128]
            vx[p, 0:288, 0:128] = v[:, p * 128 : (p + 1) * 128]

        def pair(p, carry):
            ca[slot + p] = pair_attention(cq[p, 0], cq[p, 1], vx[p, 0:288], None)
            return carry

        lax.fori_loop(0, 2, pair, 0)

    arrived(own_share, left_share)
    coarse(0)
    arrived(right_share, other_share)
    coarse(2)
    arrived(far_across)
    start(ofar_share)
    arrived(oleft_share, oright_share)
    coarse(4)
    arrived(far_share, ofar_share)
    coarse(6)
    heads = jnp.concatenate([ca[n] for n in range(8)], axis=1)
    projected = nn(heads, g[:, :, 192:256].reshape(D2, D2))
    mo[...] = (mo[...].astype(F32) + projected).astype(BF)
    out_merged = pltpu.make_async_copy(mo, merged_out, out_sem.at[1])
    out_merged.start()
    for copy in lab_copies + halo_copies + w_list:
        copy.wait_send()
    out_fine.wait()
    out_merged.wait()


def solution(mesh):
    nlat, nlon = mesh.shape["lat"], mesh.shape["lon"]
    order, back, sel, rowsel, colsel = constants()

    def shards(tokens, region_labels, fine_qkv, fine_proj, merge_weight, merged_qkv, merged_proj):
        any_space = pl.BlockSpec(memory_space=pl.ANY)
        vm = pltpu.VMEM
        dma = pltpu.SemaphoreType.DMA
        fine_out, merged_out = pl.pallas_call(
            functools.partial(kernel, nlat, nlon),
            out_shape=(jax.ShapeDtypeStruct((4, 4, 72, D1), BF), jax.ShapeDtypeStruct((288, D2), BF)),
            in_specs=[any_space] * 12,
            out_specs=(any_space, any_space),
            scratch_shapes=[
                vm((4, 4, 72, D1), BF),
                vm((3, 3, 4, 12, 24), jnp.int32),
                vm((D1, 3 * D1), BF),
                vm((D1, D1), BF),
                vm((4 * D1, D2), BF),
                vm((D2, 192), BF),
                vm(order.shape, BF),
                vm(back.shape, BF),
                vm(sel.shape, BF),
                vm(rowsel.shape, BF),
                vm(colsel.shape, BF),
                vm((6, ROWS, D1), BF),
                vm((6, ROWS, 128), BF),
                vm((3, 64, 384), F32),
                vm((4, 288, 128), BF),
                vm((4, 320, 256), BF),
                vm((4, 320, 256), BF),
                vm((4, 4, 304, 128), BF),
                vm((4, 4, 72, D1), BF),
                vm((4, 72, 4 * D1), F32),
                vm((8, 2, 256, D2), BF),
                vm((2, 2, 288, 128), BF),
                vm((8, 288, 128), BF),
                vm((288, D2), BF),
                dma((12,)),
                dma((8,)),
                dma((8,)),
                dma((8,)),
                dma((8,)),
                dma((20,)),
                dma((20,)),
                dma((2,)),
            ],
            compiler_params=pltpu.CompilerParams(
                collective_id=0, has_side_effects=True, vmem_limit_bytes=60 * 1024 * 1024
            ),
            cost_estimate=pl.CostEstimate(flops=10**10, bytes_accessed=2 * 10**7, transcendentals=4 * 10**6),
        )(
            tokens.reshape(4, 4, 72, D1), region_labels, fine_qkv, fine_proj, merge_weight, merged_qkv, merged_proj,
            order, back, sel, rowsel, colsel,
        )
        return fine_out.reshape(4, 12, 24, D1), merged_out.reshape(4, 6, 12, D2)

    in_specs = (
        P(None, "lat", "lon", None),
        P(None, "lat", "lon"),
        P(),
        P(),
        P(),
        P(None, "lat"),
        P("lat", None),
    )
    out_specs = (P(None, "lat", "lon", None), P(None, "lat", "lon", None))
    return jax.shard_map(shards, mesh=mesh, in_specs=in_specs, out_specs=out_specs, check_vma=False)
```

```python
import functools
import math

import jax
import jax.numpy as jnp
import numpy as np
from jax import lax
from jax.experimental import pallas as pl
from jax.experimental.pallas import tpu as pltpu
from jax.sharding import PartitionSpec as P

MESH = pl.DeviceIdType.MESH
BF = jnp.bfloat16
F32 = jnp.float32

D1 = 512
D2 = 1024
EPS = 1e-05
BIG = 1e32
COEF = 0.125 * math.log2(math.e)

ROWS = 464
LO = (0, 160, 304)
HI = (160, 304, 464)
QLO = (80, 160, 304)
QHI = (160, 304, 384)
BLOCKS = ((0, 72), (80, 72), (160, 72), (232, 72), (304, 72), (384, 72))

OWN, OTHER, LEFT, RIGHT, OLEFT, ORIGHT, FAR, OFAR = range(8)


def constants():
    order = np.zeros((304, 288), np.float32)
    rowsel = np.zeros((4, ROWS, 64), np.float32)
    colsel = np.zeros((ROWS, 384), np.float32)
    rowsel[:, :, 48] = 1.0
    colsel[:, 0] = 1.0
    for block, (start, _) in enumerate(BLOCKS):
        for lev in range(4):
            for r in range(3):
                for c in range(6):
                    at = start + lev * 18 + r * 6 + c
                    if 1 <= block <= 4:
                        order[at - 80, lev * 72 + r * 24 + (block - 1) * 6 + c] = 1.0
                    tile, col = ((0, 18 + c), (1, c), (1, 6 + c), (1, 12 + c), (1, 18 + c), (2, c))[block]
                    colsel[at] = 0.0
                    colsel[at, tile * 128 + col] = 1.0
                    for a in range(4):
                        rowsel[a, at] = 0.0
                        rowsel[a, at, (3 * a + r) * 4 + lev] = 1.0
    sel = np.zeros((288, 288), np.float32)
    for s in range(4):
        for r in range(6):
            for c in range(12):
                sel[s * 72 + r * 12 + c, (2 * r + s % 2) * 24 + 2 * c + s // 2] = 1.0
    cast = lambda v: jnp.asarray(v, BF)
    return cast(order), cast(order.T.copy()), cast(sel), cast(rowsel), cast(colsel)


def nt(a, b):
    return lax.dot_general(a, b, (((1,), (1,)), ((), ())), preferred_element_type=F32)


def nn(a, b):
    return jnp.dot(a, b, preferred_element_type=F32)


def norm(v):
    v = v - jnp.mean(v, axis=-1, keepdims=True)
    return v * lax.rsqrt(jnp.mean(v * v, axis=-1, keepdims=True) + EPS)


def pair_attention(q, kx, vx, aug):
    n = q.shape[0]
    even = lax.broadcasted_iota(jnp.int32, (n, 128), 1) < 64
    zero = jnp.zeros_like(q)
    heads = jnp.concatenate([jnp.where(even, q, zero), jnp.where(even, zero, q)], axis=0)
    if aug is not None:
        heads = jnp.concatenate([heads, jnp.concatenate([aug, aug], axis=0)], axis=1)
    s = nt(heads, kx)
    e = jnp.exp2((s - jnp.max(s, axis=-1, keepdims=True)) * COEF).astype(BF)
    o = nn(e, vx)
    return (jnp.where(even, o[:n, :128], o[n:, :128]) / jnp.where(even, o[:n, 128:], o[n:, 128:])).astype(BF)


def kernel(
    nlat, nlon,
    tok, lab, wqkv_h, wproj_h, wmerge_h, mqkv_h, mproj_h, order_h, back_h, sel_h, rowsel_h, colsel_h,
    fine_out, merged_out,
    x, lx, wqkv, wproj, wmerge, order, back, sel, rowsel, colsel,
    ext, aug, keys, values, queries, lf, at, fo, mn, g, ca, mo,
    load_sem, lab_send, lab_recv, halo_send, halo_recv, w_send, w_recv, out_sem,
):
    i, j = lax.axis_index("lat"), lax.axis_index("lon")
    up, down = (i + nlat - 1) % nlat, (i + 1) % nlat
    west, east = (j + nlon - 1) % nlon, (j + 1) % nlon
    core = i % 2
    chip = (i // 2) % 4
    ylo = i // 8
    partner = i + 1 - 2 * core
    xl = ylo * 8 + ((chip + 3) % 4) * 2 + core
    xr = ylo * 8 + ((chip + 1) % 4) * 2 + core
    yo = (i + 8) % nlat
    jo = (j + 8) % nlon
    zl, zr = (j // 8) * 8 + (j + 7) % 8, (j // 8) * 8 + (j + 1) % 8

    around = [(up, j), (down, j), (i, west), (i, east), (up, west), (up, east), (down, west), (down, east)]
    opposite = [1, 0, 3, 2, 7, 6, 5, 4]
    barrier = pltpu.get_barrier_semaphore()
    others = around + [(xl, j), (xr, j), (yo, j), (yo, jo), (i, zl), (i, zr)]
    for other in others:
        pl.semaphore_signal(barrier, inc=1, device_id=other, device_id_type=MESH)

    loads = [
        pltpu.make_async_copy(src, dst, load_sem.at[n])
        for n, (src, dst) in enumerate([
            (tok.at[:, 1], x.at[:, 1]), (order_h, order), (lab, lx.at[1, 1]),
            (mqkv_h, g.at[OWN, 0, pl.ds(0, 192)]), (mproj_h, g.at[OWN, 0, pl.ds(192, 64)]), (tok.at[:, 0], x.at[:, 0]), (tok.at[:, 3], x.at[:, 3]),
            (tok.at[:, 2], x.at[:, 2]), (rowsel_h, rowsel), (colsel_h, colsel), (wqkv_h, wqkv), (back_h, back), (sel_h, sel),
            (wproj_h, wproj), (wmerge_h, wmerge),
        ])
    ]
    for copy in loads:
        copy.start()
    tok1, l_order, l_lab, l_mqkv, l_mproj, tok0, tok3, tok2, l_rowsel, l_colsel, l_wqkv, l_back, l_sel, l_wproj, l_wmerge = loads
    l_tok = (tok0, tok1, tok2, tok3)

    def remote(src, dst, send, recv, device):
        return pltpu.make_async_remote_copy(
            src_ref=src, dst_ref=dst, send_sem=send, recv_sem=recv, device_id=device, device_id_type=MESH
        )

    lower, upper = pl.ds(0, 128), pl.ds(128, 128)
    odd = j % 2
    mine, rest = pl.ds(pl.multiple_of(odd * 128, 128), 128), pl.ds(pl.multiple_of((1 - odd) * 128, 128), 128)
    mine_a, mine_b = pl.ds(pl.multiple_of(odd * 128, 64), 64), pl.ds(pl.multiple_of(odd * 128 + 64, 64), 64)
    w_list = []

    def weights(src, dst, rows, device):
        n = len(w_list)
        w_list.append(remote(g.at[src, 0, rows], g.at[dst, 0, rows], w_send.at[n], w_recv.at[n], device))
        return w_list[-1]

    def share(slot):
        n = len(w_list)
        w_list.append(remote(g.at[slot, 0], g.at[slot, 1], w_send.at[n], w_recv.at[n], (partner, j)))
        return w_list[-1]

    to_xl, to_xr, to_y, to_yy, to_zl, to_zr = (xl, j), (xr, j), (yo, j), (yo, jo), (i, zl), (i, zr)
    near = [weights(OWN, LEFT, mine, to_xr), weights(OWN, RIGHT, mine, to_xl)]
    other = [weights(OWN, OTHER, lower, to_y), weights(OWN, OTHER, upper, to_yy)]
    near_rest = [weights(OWN, LEFT, rest, to_xr), weights(OWN, RIGHT, rest, to_xl)]
    far = [weights(LEFT, FAR, mine_a, to_xr), weights(RIGHT, FAR, mine_b, to_xl)]
    across = [
        weights(src, dst, rows, device)
        for src, dst in ((LEFT, OLEFT), (RIGHT, ORIGHT))
        for rows, device in ((mine_a, to_y), (mine_b, to_yy))
    ]
    far_across = [weights(FAR, OFAR, mine_a, to_y), weights(FAR, OFAR, mine_b, to_yy)]
    along = {
        slot: [weights(slot, slot, mine_a, to_zr), weights(slot, slot, mine_b, to_zl)] for slot in (OLEFT, ORIGHT, FAR, OFAR)
    }
    shares = [share(slot) for slot in range(8)]

    def start(*copies):
        for copy in copies:
            copy.start()

    def arrived(*copies):
        for copy in copies:
            copy.wait_recv()

    pl.semaphore_wait(barrier, len(others))
    places = [(2, 1), (0, 1), (1, 2), (1, 0), (2, 2), (2, 0), (0, 2), (0, 0)]
    lab_copies = [
        remote(lx.at[1, 1], lx.at[places[n][0], places[n][1]], lab_send.at[n], lab_recv.at[n], around[n]) for n in range(8)
    ]
    l_lab.wait()
    start(*lab_copies)
    l_mqkv.wait()
    l_mproj.wait()
    start(*near, *other, shares[OWN])

    halo_copies = []

    def halo(src, dst, device):
        n = len(halo_copies)
        halo_copies.append(remote(src, dst, halo_send.at[n], halo_recv.at[n], device))
        return halo_copies[-1]

    own, first, last = pl.ds(80, 304), pl.ds(80, 80), pl.ds(304, 80)
    to_east, to_west = pl.ds(384, 80), pl.ds(0, 80)
    l_order.wait()
    lon_copies, lat_copies = [], []
    for a in (1, 0, 3, 2):
        l_tok[a].wait()
        rows = x[:, a].reshape(288, D1).astype(F32)
        ext[a + 1, 80:384] = nn(order[...], norm(rows).astype(BF)).astype(BF)
        lon_copies.append(halo(ext.at[a + 1, first], ext.at[a + 1, to_east], (i, west)))
        lon_copies.append(halo(ext.at[a + 1, last], ext.at[a + 1, to_west], (i, east)))
        start(*lon_copies[-2:])
        if a in (0, 3):
            source, target, device = ((1, 5, (up, j)), None, None, (4, 0, (down, j)))[a]
            lat_copies.append(halo(ext.at[source, own], ext.at[target, own], device))
            start(lat_copies[-1])
    corner_copies = [
        halo(ext.at[source, columns], ext.at[target, columns], device)
        for source, target, device in ((1, 5, (up, j)), (4, 0, (down, j)))
        for columns in (to_west, to_east)
    ]

    def window_keys(a, a_rows, t_lat, seam):
        codes = nn(rowsel[a_rows], lf[t_lat].astype(BF)) * colsel[...].astype(F32)
        codes = nn(codes.astype(BF), jnp.ones((384, 128), BF)) + seam
        lanes = lax.broadcasted_iota(jnp.int32, (ROWS, 128), 1).astype(F32)
        aug[a] = jnp.where(codes == lanes, 1.0, 0.0).astype(BF)

    lf[...] = jnp.full(lf.shape, 7.0, F32)

    def labels_of(t_lat, t_lon):
        for row in ((9, 10, 11), range(12), (0, 1, 2))[t_lat]:
            lf[t_lat, row * 4 : row * 4 + 4, t_lon * 128 : t_lon * 128 + 24] = lx[t_lat, t_lon, row].astype(F32)

    l_rowsel.wait()
    l_colsel.wait()
    l_wqkv.wait()
    arrived(*lab_copies)
    for t_lat in range(3):
        for t_lon in range(3):
            labels_of(t_lat, t_lon)
    first_row = jnp.where(i == 0, 3.0, 0.0)
    last_row = jnp.where(i == nlat - 1, 3.0, 0.0)
    for a, (a_rows, t_lat, seam) in enumerate(
        [(3, 0, 0.0), (0, 1, first_row), (1, 1, 0.0), (2, 1, 0.0), (3, 1, 0.0), (0, 2, last_row)]
    ):
        window_keys(a, a_rows, t_lat, seam)


    def project(rows, places):
        k = nn(rows, wqkv[:, D1 : 2 * D1]).astype(BF)
        v = nn(rows, wqkv[:, 2 * D1 :]).astype(BF)
        at_row = 0
        for a, lo, hi in places:
            keys[a, lo:hi] = k[at_row : at_row + hi - lo]
            values[a, lo:hi] = v[at_row : at_row + hi - lo]
            at_row += hi - lo

    def project_own(a, carry):
        rows = ext[a + 1, 80:384]
        queries[a] = nn(rows, wqkv[:, 0:D1]).astype(BF)
        keys[a + 1, 80:384] = nn(rows, wqkv[:, D1 : 2 * D1]).astype(BF)
        values[a + 1, 80:384] = nn(rows, wqkv[:, 2 * D1 :]).astype(BF)
        return carry

    def window(u, v):
        lo, hi = LO[v], HI[v]
        ones = jnp.ones((2 * (hi - lo), 128), BF)
        both = lambda ref, lanes: jnp.concatenate([ref[2 * u, lo:hi, lanes], ref[2 * u + 1, lo:hi, lanes]], axis=0)
        marks = both(aug, slice(None))
        own_rows = ((1,), (2, 3), (4,))[u]
        qlo, qhi = QLO[v] - 80, QHI[v] - 80
        each = qhi - qlo
        q_marks = jnp.concatenate([aug[a, qlo + 80 : qhi + 80] for a in own_rows], axis=0)
        q_marks = ((q_marks.astype(F32) - 1.0) * BIG).astype(BF)
        for p in range(4):
            lanes = slice(p * 128, (p + 1) * 128)
            out = pair_attention(
                jnp.concatenate([queries[a - 1, qlo:qhi, lanes] for a in own_rows], axis=0),
                jnp.concatenate([both(keys, lanes), marks], axis=1),
                jnp.concatenate([both(values, lanes), ones], axis=1),
                q_marks,
            )
            for n, a in enumerate(own_rows):
                at[p, a - 1, qlo:qhi] = out[n * each : (n + 1) * each]

    lax.fori_loop(0, 4, project_own, 0, unroll=True)
    window(1, 1)
    arrived(*near)
    start(*far, *across, *near_rest)
    arrived(*lat_copies)
    project(ext[0, 80:384], [(0, 80, 384)])
    project(ext[5, 80:384], [(5, 80, 384)])
    window(0, 1)
    window(2, 1)
    arrived(*lon_copies)
    start(*corner_copies)
    project(ext[1:5, 0:80].reshape(320, D1), [(a, 0, 80) for a in range(1, 5)])
    window(1, 0)
    project(ext[1:5, 384:464].reshape(320, D1), [(a, 384, 464) for a in range(1, 5)])
    window(1, 2)
    arrived(*across, *far)
    start(*far_across, *along[OLEFT], *along[ORIGHT], *along[FAR])
    arrived(*corner_copies)
    edges = [(0, 0, 80), (0, 384, 464), (5, 0, 80), (5, 384, 464)]
    project(jnp.concatenate([ext[a, lo:hi] for a, lo, hi in edges], axis=0), edges)
    window(0, 0)
    window(0, 2)
    window(2, 0)
    window(2, 2)

    arrived(*far_across)
    start(*along[OFAR])
    l_back.wait()
    l_wproj.wait()

    def finish(a, carry):
        heads = jnp.concatenate([at[p, a] for p in range(4)], axis=1)
        update = nn(heads, wproj[...]).astype(BF)
        natural = nn(back[...], update).reshape(4, 72, D1)
        fo[:, a] = (x[:, a].astype(F32) + natural).astype(BF)
        return carry

    lax.fori_loop(0, 4, finish, 0, unroll=True)
    out_fine = pltpu.make_async_copy(fo, fine_out, out_sem.at[0])
    out_fine.start()

    arrived(*other, *near_rest)
    start(shares[OTHER], shares[LEFT], shares[RIGHT])

    l_sel.wait()

    def merge(lev, carry):
        parts = nn(sel[...], fo[lev].reshape(288, D1))
        cat = jnp.concatenate([parts[s * 72 : (s + 1) * 72] for s in range(4)], axis=1)
        cat = norm(cat)
        for n in range(16):
            mn[n, pl.ds(lev, 72, stride=4)] = cat[:, n * 128 : (n + 1) * 128]
        return carry

    lax.fori_loop(0, 4, merge, 0, unroll=True)
    l_wmerge.wait()
    merged_in = nn(jnp.concatenate([mn[n].astype(BF) for n in range(16)], axis=1), wmerge[...]).astype(BF)
    mo[...] = merged_in
    normed = norm(merged_in.astype(F32)).astype(BF)

    def coarse(slot):
        take = lambda lo: g[slot : slot + 2, :, lo : lo + 64].reshape(256, D2)
        q = nt(normed, take(0)).astype(BF)
        k = nt(normed, take(64)).astype(BF)
        v = nt(normed, take(128)).astype(BF)
        ones = jnp.ones((288, 128), BF)
        for p in range(2):
            lanes = slice(p * 128, (p + 1) * 128)
            ca[slot + p] = pair_attention(q[:, lanes], k[:, lanes], jnp.concatenate([v[:, lanes], ones], axis=1), None)

    for slot in (0, 2, 4, 6):
        if slot == 2:
            arrived(*along[OLEFT], *along[ORIGHT])
            start(shares[OLEFT], shares[ORIGHT])
        if slot == 4:
            arrived(*along[FAR], *along[OFAR])
            start(shares[FAR], shares[OFAR])
        arrived(shares[slot], shares[slot + 1])
        coarse(slot)
    heads = jnp.concatenate([ca[n] for n in range(8)], axis=1)
    projected = nn(heads, g[:, :, 192:256].reshape(D2, D2))
    mo[...] = (mo[...].astype(F32) + projected).astype(BF)
    out_merged = pltpu.make_async_copy(mo, merged_out, out_sem.at[1])
    out_merged.start()
    for copy in lab_copies + halo_copies + w_list:
        copy.wait_send()
    out_fine.wait()
    out_merged.wait()


def solution(mesh):
    nlat, nlon = mesh.shape["lat"], mesh.shape["lon"]
    order, back, sel, rowsel, colsel = constants()

    def shards(tokens, region_labels, fine_qkv, fine_proj, merge_weight, merged_qkv, merged_proj):
        any_space = pl.BlockSpec(memory_space=pl.ANY)
        vm = pltpu.VMEM
        dma = pltpu.SemaphoreType.DMA
        fine_out, merged_out = pl.pallas_call(
            functools.partial(kernel, nlat, nlon),
            out_shape=(jax.ShapeDtypeStruct((4, 4, 72, D1), BF), jax.ShapeDtypeStruct((288, D2), BF)),
            in_specs=[any_space] * 12,
            out_specs=(any_space, any_space),
            scratch_shapes=[
                vm((4, 4, 72, D1), BF),
                vm((3, 3, 12, 4, 24), jnp.int32),
                vm((D1, 3 * D1), BF),
                vm((D1, D1), BF),
                vm((4 * D1, D2), BF),
                vm(order.shape, BF),
                vm(back.shape, BF),
                vm(sel.shape, BF),
                vm(rowsel.shape, BF),
                vm(colsel.shape, BF),
                vm((6, ROWS, D1), BF),
                vm((6, ROWS, 128), BF),
                vm((6, ROWS, D1), BF),
                vm((6, ROWS, D1), BF),
                vm((4, 304, D1), BF),
                vm((3, 64, 384), F32),
                vm((4, 4, 304, 128), BF),
                vm((4, 4, 72, D1), BF),
                vm((16, 288, 128), F32),
                vm((8, 2, 256, D2), BF),
                vm((8, 288, 128), BF),
                vm((288, D2), BF),
                dma((15,)),
                dma((8,)),
                dma((8,)),
                dma((14,)),
                dma((14,)),
                dma((30,)),
                dma((30,)),
                dma((2,)),
            ],
            compiler_params=pltpu.CompilerParams(
                collective_id=0, has_side_effects=True, vmem_limit_bytes=60 * 1024 * 1024
            ),
            cost_estimate=pl.CostEstimate(flops=10**10, bytes_accessed=2 * 10**7, transcendentals=4 * 10**6),
        )(
            tokens.reshape(4, 4, 72, D1), region_labels.transpose(1, 0, 2), fine_qkv, fine_proj, merge_weight, merged_qkv.T, merged_proj,
            order, back, sel, rowsel, colsel,
        )
        return fine_out.reshape(4, 12, 24, D1), merged_out.reshape(6, 12, 4, D2).transpose(2, 0, 1, 3)

    in_specs = (
        P(None, "lat", "lon", None),
        P(None, "lat", "lon"),
        P(),
        P(),
        P(),
        P(None, "lat"),
        P("lat", None),
    )
    out_specs = (P(None, "lat", "lon", None), P(None, "lat", "lon", None))
    return jax.shard_map(shards, mesh=mesh, in_specs=in_specs, out_specs=out_specs, check_vma=False)
```

```python
import functools
import math

import jax
import jax.numpy as jnp
import numpy as np
from jax import lax
from jax.experimental import pallas as pl
from jax.experimental.pallas import tpu as pltpu
from jax.sharding import PartitionSpec as P

MESH = pl.DeviceIdType.MESH
BF = jnp.bfloat16
F32 = jnp.float32

D1 = 512
D2 = 1024
EPS = 1e-05
BIG = 1e32
COEF = 0.125 * math.log2(math.e)

ROWS = 464
LO = (0, 160, 304)
HI = (160, 304, 464)
QLO = (80, 160, 304)
QHI = (160, 304, 384)
BLOCKS = ((0, 72), (80, 72), (160, 72), (232, 72), (304, 72), (384, 72))

OWN, OTHER, LEFT, RIGHT, OLEFT, ORIGHT, FAR, OFAR = range(8)


def constants():
    order = np.zeros((304, 288), np.float32)
    rowsel = np.zeros((4, ROWS, 64), np.float32)
    colsel = np.zeros((ROWS, 384), np.float32)
    rowsel[:, :, 48] = 1.0
    colsel[:, 0] = 1.0
    for block, (start, _) in enumerate(BLOCKS):
        for lev in range(4):
            for r in range(3):
                for c in range(6):
                    at = start + lev * 18 + r * 6 + c
                    if 1 <= block <= 4:
                        order[at - 80, lev * 72 + r * 24 + (block - 1) * 6 + c] = 1.0
                    tile, col = ((0, 18 + c), (1, c), (1, 6 + c), (1, 12 + c), (1, 18 + c), (2, c))[block]
                    colsel[at] = 0.0
                    colsel[at, tile * 128 + col] = 1.0
                    for a in range(4):
                        rowsel[a, at] = 0.0
                        rowsel[a, at, (3 * a + r) * 4 + lev] = 1.0
    sel = np.zeros((288, 288), np.float32)
    for s in range(4):
        for r in range(6):
            for c in range(12):
                sel[s * 72 + r * 12 + c, (2 * r + s % 2) * 24 + 2 * c + s // 2] = 1.0
    cast = lambda v: jnp.asarray(v, BF)
    return cast(order), cast(order.T.copy()), cast(sel), cast(rowsel), cast(colsel)


def nt(a, b):
    return lax.dot_general(a, b, (((1,), (1,)), ((), ())), preferred_element_type=F32)


def nn(a, b):
    return jnp.dot(a, b, preferred_element_type=F32)


def norm(v):
    v = v - jnp.mean(v, axis=-1, keepdims=True)
    return v * lax.rsqrt(jnp.mean(v * v, axis=-1, keepdims=True) + EPS)


def pair_attention(q, kx, vx, aug):
    n = q.shape[0]
    even = lax.broadcasted_iota(jnp.int32, (n, 128), 1) < 64
    zero = jnp.zeros_like(q)
    heads = jnp.concatenate([jnp.where(even, q, zero), jnp.where(even, zero, q)], axis=0)
    if aug is not None:
        heads = jnp.concatenate([heads, jnp.concatenate([aug, aug], axis=0)], axis=1)
    s = nt(heads, kx)
    e = jnp.exp2((s - jnp.max(s, axis=-1, keepdims=True)) * COEF).astype(BF)
    o = nn(e, vx)
    return (jnp.where(even, o[:n, :128], o[n:, :128]) / jnp.where(even, o[:n, 128:], o[n:, 128:])).astype(BF)


def kernel(
    nlat, nlon,
    tok, lab, wqkv_h, wproj_h, wmerge_h, mqkv_h, mproj_h, order_h, back_h, sel_h, rowsel_h, colsel_h,
    fine_out, merged_out,
    x, lx, wqkv, wproj, wmerge, order, back, sel, rowsel, colsel,
    ext, aug, keys, values, queries, lf, at, fo, mn, g, ca, mo,
    load_sem, lab_send, lab_recv, halo_send, halo_recv, w_send, w_recv, out_sem,
):
    i, j = lax.axis_index("lat"), lax.axis_index("lon")
    up, down = (i + nlat - 1) % nlat, (i + 1) % nlat
    west, east = (j + nlon - 1) % nlon, (j + 1) % nlon
    core = i % 2
    chip = (i // 2) % 4
    ylo = i // 8
    partner = i + 1 - 2 * core
    xl = ylo * 8 + ((chip + 3) % 4) * 2 + core
    xr = ylo * 8 + ((chip + 1) % 4) * 2 + core
    yo = (i + 8) % nlat
    jo = (j + 8) % nlon
    zl, zr = (j // 8) * 8 + (j + 7) % 8, (j // 8) * 8 + (j + 1) % 8

    around = [(up, j), (down, j), (i, west), (i, east), (up, west), (up, east), (down, west), (down, east)]
    opposite = [1, 0, 3, 2, 7, 6, 5, 4]
    barrier = pltpu.get_barrier_semaphore()
    others = around + [(xl, j), (xr, j), (yo, j), (yo, jo), (i, zl), (i, zr)]
    for other in others:
        pl.semaphore_signal(barrier, inc=1, device_id=other, device_id_type=MESH)

    loads = [
        pltpu.make_async_copy(src, dst, load_sem.at[n])
        for n, (src, dst) in enumerate([
            (tok.at[:, 1], x.at[:, 1]), (order_h, order), (lab, lx.at[1, 1]),
            (mqkv_h, g.at[OWN, 0, pl.ds(0, 192)]), (mproj_h, g.at[OWN, 0, pl.ds(192, 64)]), (tok.at[:, 0], x.at[:, 0]), (tok.at[:, 3], x.at[:, 3]),
            (tok.at[:, 2], x.at[:, 2]), (rowsel_h, rowsel), (colsel_h, colsel), (wqkv_h, wqkv), (back_h, back), (sel_h, sel),
            (wproj_h, wproj), (wmerge_h, wmerge),
        ])
    ]
    for copy in loads:
        copy.start()
    tok1, l_order, l_lab, l_mqkv, l_mproj, tok0, tok3, tok2, l_rowsel, l_colsel, l_wqkv, l_back, l_sel, l_wproj, l_wmerge = loads
    l_tok = (tok0, tok1, tok2, tok3)

    def remote(src, dst, send, recv, device):
        return pltpu.make_async_remote_copy(
            src_ref=src, dst_ref=dst, send_sem=send, recv_sem=recv, device_id=device, device_id_type=MESH
        )

    lower, upper = pl.ds(0, 128), pl.ds(128, 128)
    odd = j % 2
    mine, rest = pl.ds(pl.multiple_of(odd * 128, 128), 128), pl.ds(pl.multiple_of((1 - odd) * 128, 128), 128)
    mine_a, mine_b = pl.ds(pl.multiple_of(odd * 128, 64), 64), pl.ds(pl.multiple_of(odd * 128 + 64, 64), 64)
    w_list = []

    def weights(src, dst, rows, device):
        n = len(w_list)
        w_list.append(remote(g.at[src, 0, rows], g.at[dst, 0, rows], w_send.at[n], w_recv.at[n], device))
        return w_list[-1]

    def share(slot):
        n = len(w_list)
        w_list.append(remote(g.at[slot, 0], g.at[slot, 1], w_send.at[n], w_recv.at[n], (partner, j)))
        return w_list[-1]

    to_xl, to_xr, to_y, to_yy, to_zl, to_zr = (xl, j), (xr, j), (yo, j), (yo, jo), (i, zl), (i, zr)
    near = [weights(OWN, LEFT, mine, to_xr), weights(OWN, RIGHT, mine, to_xl)]
    other = [weights(OWN, OTHER, lower, to_y), weights(OWN, OTHER, upper, to_yy)]
    near_rest = [weights(OWN, LEFT, rest, to_xr), weights(OWN, RIGHT, rest, to_xl)]
    far = [weights(LEFT, FAR, mine_a, to_xr), weights(RIGHT, FAR, mine_b, to_xl)]
    across = [
        weights(src, dst, rows, device)
        for src, dst in ((LEFT, OLEFT), (RIGHT, ORIGHT))
        for rows, device in ((mine_a, to_y), (mine_b, to_yy))
    ]
    far_across = [weights(FAR, OFAR, mine_a, to_y), weights(FAR, OFAR, mine_b, to_yy)]
    along = {
        slot: [weights(slot, slot, mine_a, to_zr), weights(slot, slot, mine_b, to_zl)] for slot in (OLEFT, ORIGHT, FAR, OFAR)
    }
    shares = [share(slot) for slot in range(8)]

    def start(*copies):
        for copy in copies:
            copy.start()

    def arrived(*copies):
        for copy in copies:
            copy.wait_recv()

    pl.semaphore_wait(barrier, len(others))
    places = [(2, 1), (0, 1), (1, 2), (1, 0), (2, 2), (2, 0), (0, 2), (0, 0)]
    lab_copies = [
        remote(lx.at[1, 1], lx.at[places[n][0], places[n][1]], lab_send.at[n], lab_recv.at[n], around[n]) for n in range(8)
    ]
    l_lab.wait()
    start(*lab_copies)
    l_mqkv.wait()
    l_mproj.wait()
    start(*near, shares[OWN])

    halo_copies = []

    def halo(src, dst, device):
        n = len(halo_copies)
        halo_copies.append(remote(src, dst, halo_send.at[n], halo_recv.at[n], device))
        return halo_copies[-1]

    own, first, last = pl.ds(80, 304), pl.ds(80, 80), pl.ds(304, 80)
    to_east, to_west = pl.ds(384, 80), pl.ds(0, 80)
    l_order.wait()
    lon_copies, lat_copies = [], []
    for a in (1, 0, 3, 2):
        l_tok[a].wait()
        rows = x[:, a].reshape(288, D1).astype(F32)
        ext[a + 1, 80:384] = nn(order[...], norm(rows).astype(BF)).astype(BF)
        lon_copies.append(halo(ext.at[a + 1, first], ext.at[a + 1, to_east], (i, west)))
        lon_copies.append(halo(ext.at[a + 1, last], ext.at[a + 1, to_west], (i, east)))
        start(*lon_copies[-2:])
        if a in (0, 3):
            source, target, device = ((1, 5, (up, j)), None, None, (4, 0, (down, j)))[a]
            lat_copies.append(halo(ext.at[source, own], ext.at[target, own], device))
            start(lat_copies[-1])
    corner_copies = [
        halo(ext.at[source, columns], ext.at[target, columns], device)
        for source, target, device in ((1, 5, (up, j)), (4, 0, (down, j)))
        for columns in (to_west, to_east)
    ]

    def window_keys(a, a_rows, t_lat, seam):
        codes = nn(rowsel[a_rows], lf[t_lat].astype(BF)) * colsel[...].astype(F32)
        codes = nn(codes.astype(BF), jnp.ones((384, 128), BF)) + seam
        lanes = lax.broadcasted_iota(jnp.int32, (ROWS, 128), 1).astype(F32)
        aug[a] = jnp.where(codes == lanes, 1.0, 0.0).astype(BF)

    lf[...] = jnp.full(lf.shape, 7.0, F32)

    def labels_of(t_lat, t_lon):
        for row in ((9, 10, 11), range(12), (0, 1, 2))[t_lat]:
            lf[t_lat, row * 4 : row * 4 + 4, t_lon * 128 : t_lon * 128 + 24] = lx[t_lat, t_lon, row].astype(F32)

    l_rowsel.wait()
    l_colsel.wait()
    l_wqkv.wait()
    arrived(*lab_copies)
    for t_lat in range(3):
        for t_lon in range(3):
            labels_of(t_lat, t_lon)
    first_row = jnp.where(i == 0, 3.0, 0.0)
    last_row = jnp.where(i == nlat - 1, 3.0, 0.0)
    for a, (a_rows, t_lat, seam) in enumerate(
        [(3, 0, 0.0), (0, 1, first_row), (1, 1, 0.0), (2, 1, 0.0), (3, 1, 0.0), (0, 2, last_row)]
    ):
        window_keys(a, a_rows, t_lat, seam)


    def project(rows, places):
        k = nn(rows, wqkv[:, D1 : 2 * D1]).astype(BF)
        v = nn(rows, wqkv[:, 2 * D1 :]).astype(BF)
        at_row = 0
        for a, lo, hi in places:
            keys[a, lo:hi] = k[at_row : at_row + hi - lo]
            values[a, lo:hi] = v[at_row : at_row + hi - lo]
            at_row += hi - lo

    def project_own(a, carry):
        rows = ext[a + 1, 80:384]
        queries[a] = nn(rows, wqkv[:, 0:D1]).astype(BF)
        keys[a + 1, 80:384] = nn(rows, wqkv[:, D1 : 2 * D1]).astype(BF)
        values[a + 1, 80:384] = nn(rows, wqkv[:, 2 * D1 :]).astype(BF)
        return carry

    def window(u, v):
        lo, hi = LO[v], HI[v]
        ones = jnp.ones((2 * (hi - lo), 128), BF)
        both = lambda ref, lanes: jnp.concatenate([ref[2 * u, lo:hi, lanes], ref[2 * u + 1, lo:hi, lanes]], axis=0)
        marks = both(aug, slice(None))
        own_rows = ((1,), (2, 3), (4,))[u]
        qlo, qhi = QLO[v] - 80, QHI[v] - 80
        each = qhi - qlo
        q_marks = jnp.concatenate([aug[a, qlo + 80 : qhi + 80] for a in own_rows], axis=0)
        q_marks = ((q_marks.astype(F32) - 1.0) * BIG).astype(BF)
        for p in range(4):
            lanes = slice(p * 128, (p + 1) * 128)
            out = pair_attention(
                jnp.concatenate([queries[a - 1, qlo:qhi, lanes] for a in own_rows], axis=0),
                jnp.concatenate([both(keys, lanes), marks], axis=1),
                jnp.concatenate([both(values, lanes), ones], axis=1),
                q_marks,
            )
            for n, a in enumerate(own_rows):
                at[p, a - 1, qlo:qhi] = out[n * each : (n + 1) * each]

    lax.fori_loop(0, 4, project_own, 0, unroll=True)
    window(1, 1)
    arrived(*near)
    start(*far, *across)
    arrived(*lat_copies)
    project(ext[0, 80:384], [(0, 80, 384)])
    project(ext[5, 80:384], [(5, 80, 384)])
    window(0, 1)
    window(2, 1)
    arrived(*lon_copies)
    start(*corner_copies)
    project(ext[1:5, 0:80].reshape(320, D1), [(a, 0, 80) for a in range(1, 5)])
    window(1, 0)
    project(ext[1:5, 384:464].reshape(320, D1), [(a, 384, 464) for a in range(1, 5)])
    window(1, 2)
    arrived(*across, *far)
    start(*far_across, *along[OLEFT], *along[ORIGHT], *along[FAR])
    arrived(*corner_copies)
    start(*near_rest, *other)
    edges = [(0, 0, 80), (0, 384, 464), (5, 0, 80), (5, 384, 464)]
    project(jnp.concatenate([ext[a, lo:hi] for a, lo, hi in edges], axis=0), edges)
    window(0, 0)
    window(0, 2)
    window(2, 0)
    window(2, 2)

    arrived(*far_across)
    start(*along[OFAR])
    l_back.wait()
    l_wproj.wait()

    def finish(a, carry):
        heads = jnp.concatenate([at[p, a] for p in range(4)], axis=1)
        update = nn(heads, wproj[...]).astype(BF)
        natural = nn(back[...], update).reshape(4, 72, D1)
        fo[:, a] = (x[:, a].astype(F32) + natural).astype(BF)
        return carry

    lax.fori_loop(0, 4, finish, 0, unroll=True)
    out_fine = pltpu.make_async_copy(fo, fine_out, out_sem.at[0])
    out_fine.start()


    l_sel.wait()

    def merge(lev, carry):
        parts = nn(sel[...], fo[lev].reshape(288, D1))
        cat = jnp.concatenate([parts[s * 72 : (s + 1) * 72] for s in range(4)], axis=1)
        cat = norm(cat)
        for n in range(16):
            mn[n, pl.ds(lev, 72, stride=4)] = cat[:, n * 128 : (n + 1) * 128]
        return carry

    lax.fori_loop(0, 4, merge, 0, unroll=True)
    l_wmerge.wait()
    merged_in = nn(jnp.concatenate([mn[n].astype(BF) for n in range(16)], axis=1), wmerge[...]).astype(BF)
    mo[...] = merged_in
    normed = norm(merged_in.astype(F32)).astype(BF)

    def coarse(slot):
        take = lambda lo: g[slot : slot + 2, :, lo : lo + 64].reshape(256, D2)
        q = nt(normed, take(0)).astype(BF)
        k = nt(normed, take(64)).astype(BF)
        v = nt(normed, take(128)).astype(BF)
        ones = jnp.ones((288, 128), BF)
        for p in range(2):
            lanes = slice(p * 128, (p + 1) * 128)
            ca[slot + p] = pair_attention(q[:, lanes], k[:, lanes], jnp.concatenate([v[:, lanes], ones], axis=1), None)

    arrived(*other, *near_rest)
    start(shares[OTHER], shares[LEFT], shares[RIGHT])
    for slot in (0, 2, 4, 6):
        if slot == 2:
            arrived(*along[OLEFT], *along[ORIGHT])
            start(shares[OLEFT], shares[ORIGHT])
        if slot == 4:
            arrived(*along[FAR], *along[OFAR])
            start(shares[FAR], shares[OFAR])
        arrived(shares[slot], shares[slot + 1])
        coarse(slot)
    heads = jnp.concatenate([ca[n] for n in range(8)], axis=1)
    projected = nn(heads, g[:, :, 192:256].reshape(D2, D2))
    mo[...] = (mo[...].astype(F32) + projected).astype(BF)
    out_merged = pltpu.make_async_copy(mo, merged_out, out_sem.at[1])
    out_merged.start()
    for copy in lab_copies + halo_copies + w_list:
        copy.wait_send()
    out_fine.wait()
    out_merged.wait()


def solution(mesh):
    nlat, nlon = mesh.shape["lat"], mesh.shape["lon"]
    order, back, sel, rowsel, colsel = constants()

    def shards(tokens, region_labels, fine_qkv, fine_proj, merge_weight, merged_qkv, merged_proj):
        any_space = pl.BlockSpec(memory_space=pl.ANY)
        vm = pltpu.VMEM
        dma = pltpu.SemaphoreType.DMA
        fine_out, merged_out = pl.pallas_call(
            functools.partial(kernel, nlat, nlon),
            out_shape=(jax.ShapeDtypeStruct((4, 4, 72, D1), BF), jax.ShapeDtypeStruct((288, D2), BF)),
            in_specs=[any_space] * 12,
            out_specs=(any_space, any_space),
            scratch_shapes=[
                vm((4, 4, 72, D1), BF),
                vm((3, 3, 12, 4, 24), jnp.int32),
                vm((D1, 3 * D1), BF),
                vm((D1, D1), BF),
                vm((4 * D1, D2), BF),
                vm(order.shape, BF),
                vm(back.shape, BF),
                vm(sel.shape, BF),
                vm(rowsel.shape, BF),
                vm(colsel.shape, BF),
                vm((6, ROWS, D1), BF),
                vm((6, ROWS, 128), BF),
                vm((6, ROWS, D1), BF),
                vm((6, ROWS, D1), BF),
                vm((4, 304, D1), BF),
                vm((3, 64, 384), F32),
                vm((4, 4, 304, 128), BF),
                vm((4, 4, 72, D1), BF),
                vm((16, 288, 128), F32),
                vm((8, 2, 256, D2), BF),
                vm((8, 288, 128), BF),
                vm((288, D2), BF),
                dma((15,)),
                dma((8,)),
                dma((8,)),
                dma((14,)),
                dma((14,)),
                dma((30,)),
                dma((30,)),
                dma((2,)),
            ],
            compiler_params=pltpu.CompilerParams(
                collective_id=0, has_side_effects=True, vmem_limit_bytes=60 * 1024 * 1024
            ),
            cost_estimate=pl.CostEstimate(flops=10**10, bytes_accessed=2 * 10**7, transcendentals=4 * 10**6),
        )(
            tokens.reshape(4, 4, 72, D1), region_labels.transpose(1, 0, 2), fine_qkv, fine_proj, merge_weight, merged_qkv.T, merged_proj,
            order, back, sel, rowsel, colsel,
        )
        return fine_out.reshape(4, 12, 24, D1), merged_out.reshape(6, 12, 4, D2).transpose(2, 0, 1, 3)

    in_specs = (
        P(None, "lat", "lon", None),
        P(None, "lat", "lon"),
        P(),
        P(),
        P(),
        P(None, "lat"),
        P("lat", None),
    )
    out_specs = (P(None, "lat", "lon", None), P(None, "lat", "lon", None))
    return jax.shard_map(shards, mesh=mesh, in_specs=in_specs, out_specs=out_specs, check_vma=False)
```

```python
import functools
import math

import jax
import jax.numpy as jnp
import numpy as np
from jax import lax
from jax.experimental import pallas as pl
from jax.experimental.pallas import tpu as pltpu
from jax.sharding import PartitionSpec as P

MESH = pl.DeviceIdType.MESH
BF = jnp.bfloat16
F32 = jnp.float32

D1 = 512
D2 = 1024
EPS = 1e-05
BIG = 1e32
COEF = 0.125 * math.log2(math.e)

ROWS = 464
LO = (0, 160, 304)
HI = (160, 304, 464)
QLO = (80, 160, 304)
QHI = (160, 304, 384)
BLOCKS = ((0, 72), (80, 72), (160, 72), (232, 72), (304, 72), (384, 72))

OWN, LEFT, RIGHT, OLEFT, ORIGHT, FAR, OFAR, OTHER = range(8)


def constants():
    order = np.zeros((304, 288), np.float32)
    rowsel = np.zeros((4, ROWS, 64), np.float32)
    colsel = np.zeros((ROWS, 384), np.float32)
    rowsel[:, :, 48] = 1.0
    colsel[:, 0] = 1.0
    for block, (start, _) in enumerate(BLOCKS):
        for lev in range(4):
            for r in range(3):
                for c in range(6):
                    at = start + lev * 18 + r * 6 + c
                    if 1 <= block <= 4:
                        order[at - 80, lev * 72 + r * 24 + (block - 1) * 6 + c] = 1.0
                    tile, col = ((0, 18 + c), (1, c), (1, 6 + c), (1, 12 + c), (1, 18 + c), (2, c))[block]
                    colsel[at] = 0.0
                    colsel[at, tile * 128 + col] = 1.0
                    for a in range(4):
                        rowsel[a, at] = 0.0
                        rowsel[a, at, (3 * a + r) * 4 + lev] = 1.0
    sel = np.zeros((288, 288), np.float32)
    for s in range(4):
        for r in range(6):
            for c in range(12):
                sel[s * 72 + r * 12 + c, (2 * r + s % 2) * 24 + 2 * c + s // 2] = 1.0
    cast = lambda v: jnp.asarray(v, BF)
    return cast(order), cast(order.T.copy()), cast(sel), cast(rowsel), cast(colsel)


def nt(a, b):
    return lax.dot_general(a, b, (((1,), (1,)), ((), ())), preferred_element_type=F32)


def nn(a, b):
    return jnp.dot(a, b, preferred_element_type=F32)


def norm(v):
    v = v - jnp.mean(v, axis=-1, keepdims=True)
    return v * lax.rsqrt(jnp.mean(v * v, axis=-1, keepdims=True) + EPS)


def pair_attention(q, kx, vx, aug):
    n = q.shape[0]
    even = lax.broadcasted_iota(jnp.int32, (n, 128), 1) < 64
    zero = jnp.zeros_like(q)
    heads = jnp.concatenate([jnp.where(even, q, zero), jnp.where(even, zero, q)], axis=0)
    if aug is not None:
        heads = jnp.concatenate([heads, jnp.concatenate([aug, aug], axis=0)], axis=1)
    s = nt(heads, kx)
    e = jnp.exp2((s - jnp.max(s, axis=-1, keepdims=True)) * COEF).astype(BF)
    o = nn(e, vx)
    return (jnp.where(even, o[:n, :128], o[n:, :128]) / jnp.where(even, o[:n, 128:], o[n:, 128:])).astype(BF)


def kernel(
    nlat, nlon,
    tok, lab, wqkv_h, wproj_h, wmerge_h, mqkv_h, mproj_h, order_h, back_h, sel_h, rowsel_h, colsel_h,
    fine_out, merged_out,
    x, lx, wqkv, wproj, wmerge, order, back, sel, rowsel, colsel,
    ext, aug, keys, values, queries, lf, at, fo, mn, g, ca, mo,
    load_sem, lab_send, lab_recv, halo_send, halo_recv, w_send, w_recv, out_sem,
):
    i, j = lax.axis_index("lat"), lax.axis_index("lon")
    up, down = (i + nlat - 1) % nlat, (i + 1) % nlat
    west, east = (j + nlon - 1) % nlon, (j + 1) % nlon
    core = i % 2
    chip = (i // 2) % 4
    ylo = i // 8
    partner = i + 1 - 2 * core
    xl = ylo * 8 + ((chip + 3) % 4) * 2 + core
    xr = ylo * 8 + ((chip + 1) % 4) * 2 + core
    yo = (i + 8) % nlat
    jo = (j + 8) % nlon
    zl, zr = (j // 8) * 8 + (j + 7) % 8, (j // 8) * 8 + (j + 1) % 8

    around = [(up, j), (down, j), (i, west), (i, east), (up, west), (up, east), (down, west), (down, east)]
    opposite = [1, 0, 3, 2, 7, 6, 5, 4]
    barrier = pltpu.get_barrier_semaphore()
    others = around + [(xl, j), (xr, j), (yo, j), (yo, jo), (i, zl), (i, zr)]
    for other in others:
        pl.semaphore_signal(barrier, inc=1, device_id=other, device_id_type=MESH)

    loads = [
        pltpu.make_async_copy(src, dst, load_sem.at[n])
        for n, (src, dst) in enumerate([
            (tok.at[:, 1], x.at[:, 1]), (order_h, order), (lab, lx.at[1, 1]),
            (mqkv_h, g.at[OWN, 0, pl.ds(0, 192)]), (mproj_h, g.at[OWN, 0, pl.ds(192, 64)]), (tok.at[:, 0], x.at[:, 0]), (tok.at[:, 3], x.at[:, 3]),
            (tok.at[:, 2], x.at[:, 2]), (rowsel_h, rowsel), (colsel_h, colsel), (wqkv_h, wqkv), (back_h, back), (sel_h, sel),
            (wproj_h, wproj), (wmerge_h, wmerge),
        ])
    ]
    for copy in loads:
        copy.start()
    tok1, l_order, l_lab, l_mqkv, l_mproj, tok0, tok3, tok2, l_rowsel, l_colsel, l_wqkv, l_back, l_sel, l_wproj, l_wmerge = loads
    l_tok = (tok0, tok1, tok2, tok3)

    def remote(src, dst, send, recv, device):
        return pltpu.make_async_remote_copy(
            src_ref=src, dst_ref=dst, send_sem=send, recv_sem=recv, device_id=device, device_id_type=MESH
        )

    lower, upper = pl.ds(0, 128), pl.ds(128, 128)
    odd = j % 2
    mine, rest = pl.ds(pl.multiple_of(odd * 128, 128), 128), pl.ds(pl.multiple_of((1 - odd) * 128, 128), 128)
    mine_a, mine_b = pl.ds(pl.multiple_of(odd * 128, 64), 64), pl.ds(pl.multiple_of(odd * 128 + 64, 64), 64)
    w_list = []

    def weights(src, dst, rows, device):
        n = len(w_list)
        w_list.append(remote(g.at[src, 0, rows], g.at[dst, 0, rows], w_send.at[n], w_recv.at[n], device))
        return w_list[-1]

    def share(slot):
        n = len(w_list)
        w_list.append(remote(g.at[slot, 0], g.at[slot, 1], w_send.at[n], w_recv.at[n], (partner, j)))
        return w_list[-1]

    to_xl, to_xr, to_y, to_yy, to_zl, to_zr = (xl, j), (xr, j), (yo, j), (yo, jo), (i, zl), (i, zr)
    near = [weights(OWN, LEFT, mine, to_xr), weights(OWN, RIGHT, mine, to_xl)]
    other = [weights(OWN, OTHER, lower, to_y), weights(OWN, OTHER, upper, to_yy)]
    near_rest = [weights(OWN, LEFT, rest, to_xr), weights(OWN, RIGHT, rest, to_xl)]
    far = [weights(LEFT, FAR, mine_a, to_xr), weights(RIGHT, FAR, mine_b, to_xl)]
    across = [
        weights(src, dst, rows, device)
        for src, dst in ((LEFT, OLEFT), (RIGHT, ORIGHT))
        for rows, device in ((mine_a, to_y), (mine_b, to_yy))
    ]
    far_across = [weights(FAR, OFAR, mine_a, to_y), weights(FAR, OFAR, mine_b, to_yy)]
    along = {
        slot: [weights(slot, slot, mine_a, to_zr), weights(slot, slot, mine_b, to_zl)] for slot in (OLEFT, ORIGHT, FAR, OFAR)
    }
    shares = [share(slot) for slot in range(8)]

    def start(*copies):
        for copy in copies:
            copy.start()

    def arrived(*copies):
        for copy in copies:
            copy.wait_recv()

    pl.semaphore_wait(barrier, len(others))
    places = [(2, 1), (0, 1), (1, 2), (1, 0), (2, 2), (2, 0), (0, 2), (0, 0)]
    lab_copies = [
        remote(lx.at[1, 1], lx.at[places[n][0], places[n][1]], lab_send.at[n], lab_recv.at[n], around[n]) for n in range(8)
    ]
    l_lab.wait()
    start(*lab_copies)
    l_mqkv.wait()
    l_mproj.wait()
    start(*near, shares[OWN])

    halo_copies = []

    def halo(src, dst, device):
        n = len(halo_copies)
        halo_copies.append(remote(src, dst, halo_send.at[n], halo_recv.at[n], device))
        return halo_copies[-1]

    own, first, last = pl.ds(80, 304), pl.ds(80, 80), pl.ds(304, 80)
    to_east, to_west = pl.ds(384, 80), pl.ds(0, 80)
    l_order.wait()
    lon_copies, lat_copies = [], []
    for a in (1, 0, 3, 2):
        l_tok[a].wait()
        rows = x[:, a].reshape(288, D1).astype(F32)
        ext[a + 1, 80:384] = nn(order[...], norm(rows).astype(BF)).astype(BF)
        lon_copies.append(halo(ext.at[a + 1, first], ext.at[a + 1, to_east], (i, west)))
        lon_copies.append(halo(ext.at[a + 1, last], ext.at[a + 1, to_west], (i, east)))
        start(*lon_copies[-2:])
        if a in (0, 3):
            source, target, device = ((1, 5, (up, j)), None, None, (4, 0, (down, j)))[a]
            lat_copies.append(halo(ext.at[source, own], ext.at[target, own], device))
            start(lat_copies[-1])
    corner_copies = [
        halo(ext.at[source, columns], ext.at[target, columns], device)
        for source, target, device in ((1, 5, (up, j)), (4, 0, (down, j)))
        for columns in (to_west, to_east)
    ]

    def window_keys(a, a_rows, t_lat, seam):
        codes = nn(rowsel[a_rows], lf[t_lat].astype(BF)) * colsel[...].astype(F32)
        codes = nn(codes.astype(BF), jnp.ones((384, 128), BF)) + seam
        lanes = lax.broadcasted_iota(jnp.int32, (ROWS, 128), 1).astype(F32)
        aug[a] = jnp.where(codes == lanes, 1.0, 0.0).astype(BF)

    lf[...] = jnp.full(lf.shape, 7.0, F32)

    def labels_of(t_lat, t_lon):
        for row in ((9, 10, 11), range(12), (0, 1, 2))[t_lat]:
            lf[t_lat, row * 4 : row * 4 + 4, t_lon * 128 : t_lon * 128 + 24] = lx[t_lat, t_lon, row].astype(F32)

    l_rowsel.wait()
    l_colsel.wait()
    l_wqkv.wait()
    arrived(*lab_copies)
    for t_lat in range(3):
        for t_lon in range(3):
            labels_of(t_lat, t_lon)
    first_row = jnp.where(i == 0, 3.0, 0.0)
    last_row = jnp.where(i == nlat - 1, 3.0, 0.0)
    for a, (a_rows, t_lat, seam) in enumerate(
        [(3, 0, 0.0), (0, 1, first_row), (1, 1, 0.0), (2, 1, 0.0), (3, 1, 0.0), (0, 2, last_row)]
    ):
        window_keys(a, a_rows, t_lat, seam)


    def project(rows, places):
        k = nn(rows, wqkv[:, D1 : 2 * D1]).astype(BF)
        v = nn(rows, wqkv[:, 2 * D1 :]).astype(BF)
        at_row = 0
        for a, lo, hi in places:
            keys[a, lo:hi] = k[at_row : at_row + hi - lo]
            values[a, lo:hi] = v[at_row : at_row + hi - lo]
            at_row += hi - lo

    def project_own(a, carry):
        rows = ext[a + 1, 80:384]
        queries[a] = nn(rows, wqkv[:, 0:D1]).astype(BF)
        keys[a + 1, 80:384] = nn(rows, wqkv[:, D1 : 2 * D1]).astype(BF)
        values[a + 1, 80:384] = nn(rows, wqkv[:, 2 * D1 :]).astype(BF)
        return carry

    def window(u, v):
        lo, hi = LO[v], HI[v]
        ones = jnp.ones((2 * (hi - lo), 128), BF)
        both = lambda ref, lanes: jnp.concatenate([ref[2 * u, lo:hi, lanes], ref[2 * u + 1, lo:hi, lanes]], axis=0)
        marks = both(aug, slice(None))
        own_rows = ((1,), (2, 3), (4,))[u]
        qlo, qhi = QLO[v] - 80, QHI[v] - 80
        each = qhi - qlo
        q_marks = jnp.concatenate([aug[a, qlo + 80 : qhi + 80] for a in own_rows], axis=0)
        q_marks = ((q_marks.astype(F32) - 1.0) * BIG).astype(BF)
        for p in range(4):
            lanes = slice(p * 128, (p + 1) * 128)
            out = pair_attention(
                jnp.concatenate([queries[a - 1, qlo:qhi, lanes] for a in own_rows], axis=0),
                jnp.concatenate([both(keys, lanes), marks], axis=1),
                jnp.concatenate([both(values, lanes), ones], axis=1),
                q_marks,
            )
            for n, a in enumerate(own_rows):
                at[p, a - 1, qlo:qhi] = out[n * each : (n + 1) * each]

    lax.fori_loop(0, 4, project_own, 0, unroll=True)
    window(1, 1)
    arrived(*near)
    start(*far, *across)
    arrived(*lat_copies)
    project(ext[0, 80:384], [(0, 80, 384)])
    project(ext[5, 80:384], [(5, 80, 384)])
    window(0, 1)
    window(2, 1)
    arrived(*lon_copies)
    start(*corner_copies)
    project(ext[1:5, 0:80].reshape(320, D1), [(a, 0, 80) for a in range(1, 5)])
    window(1, 0)
    project(ext[1:5, 384:464].reshape(320, D1), [(a, 384, 464) for a in range(1, 5)])
    window(1, 2)
    arrived(*across, *far)
    start(*far_across, *along[OLEFT], *along[ORIGHT], *along[FAR])
    arrived(*corner_copies)
    start(*near_rest)
    edges = [(0, 0, 80), (0, 384, 464), (5, 0, 80), (5, 384, 464)]
    project(jnp.concatenate([ext[a, lo:hi] for a, lo, hi in edges], axis=0), edges)
    window(0, 0)
    window(0, 2)
    window(2, 0)
    window(2, 2)

    arrived(*far_across)
    start(*along[OFAR], *other)
    l_back.wait()
    l_wproj.wait()

    def finish(a, carry):
        heads = jnp.concatenate([at[p, a] for p in range(4)], axis=1)
        update = nn(heads, wproj[...]).astype(BF)
        natural = nn(back[...], update).reshape(4, 72, D1)
        fo[:, a] = (x[:, a].astype(F32) + natural).astype(BF)
        return carry

    lax.fori_loop(0, 4, finish, 0, unroll=True)
    out_fine = pltpu.make_async_copy(fo, fine_out, out_sem.at[0])
    out_fine.start()


    l_sel.wait()

    def merge(lev, carry):
        parts = nn(sel[...], fo[lev].reshape(288, D1))
        cat = jnp.concatenate([parts[s * 72 : (s + 1) * 72] for s in range(4)], axis=1)
        cat = norm(cat)
        for n in range(16):
            mn[n, pl.ds(lev, 72, stride=4)] = cat[:, n * 128 : (n + 1) * 128]
        return carry

    lax.fori_loop(0, 4, merge, 0, unroll=True)
    arrived(*near_rest)
    start(shares[LEFT], shares[RIGHT])
    l_wmerge.wait()
    merged_in = nn(jnp.concatenate([mn[n].astype(BF) for n in range(16)], axis=1), wmerge[...]).astype(BF)
    mo[...] = merged_in
    normed = norm(merged_in.astype(F32)).astype(BF)

    def coarse(slot):
        take = lambda lo: g[slot : slot + 2, :, lo : lo + 64].reshape(256, D2)
        q = nt(normed, take(0)).astype(BF)
        k = nt(normed, take(64)).astype(BF)
        v = nt(normed, take(128)).astype(BF)
        ones = jnp.ones((288, 128), BF)
        for p in range(2):
            lanes = slice(p * 128, (p + 1) * 128)
            ca[slot + p] = pair_attention(q[:, lanes], k[:, lanes], jnp.concatenate([v[:, lanes], ones], axis=1), None)

    arrived(*along[OLEFT], *along[ORIGHT])
    start(shares[OLEFT], shares[ORIGHT])
    arrived(shares[OWN], shares[LEFT])
    coarse(0)
    arrived(*along[FAR])
    start(shares[FAR])
    arrived(shares[RIGHT], shares[OLEFT])
    coarse(2)
    arrived(*along[OFAR], *other)
    start(shares[OFAR], shares[OTHER])
    arrived(shares[ORIGHT], shares[FAR])
    coarse(4)
    arrived(shares[OFAR], shares[OTHER])
    coarse(6)
    heads = jnp.concatenate([ca[n] for n in range(8)], axis=1)
    projected = nn(heads, g[:, :, 192:256].reshape(D2, D2))
    mo[...] = (mo[...].astype(F32) + projected).astype(BF)
    out_merged = pltpu.make_async_copy(mo, merged_out, out_sem.at[1])
    out_merged.start()
    for copy in lab_copies + halo_copies + w_list:
        copy.wait_send()
    out_fine.wait()
    out_merged.wait()


def solution(mesh):
    nlat, nlon = mesh.shape["lat"], mesh.shape["lon"]
    order, back, sel, rowsel, colsel = constants()

    def shards(tokens, region_labels, fine_qkv, fine_proj, merge_weight, merged_qkv, merged_proj):
        any_space = pl.BlockSpec(memory_space=pl.ANY)
        vm = pltpu.VMEM
        dma = pltpu.SemaphoreType.DMA
        fine_out, merged_out = pl.pallas_call(
            functools.partial(kernel, nlat, nlon),
            out_shape=(jax.ShapeDtypeStruct((4, 4, 72, D1), BF), jax.ShapeDtypeStruct((288, D2), BF)),
            in_specs=[any_space] * 12,
            out_specs=(any_space, any_space),
            scratch_shapes=[
                vm((4, 4, 72, D1), BF),
                vm((3, 3, 12, 4, 24), jnp.int32),
                vm((D1, 3 * D1), BF),
                vm((D1, D1), BF),
                vm((4 * D1, D2), BF),
                vm(order.shape, BF),
                vm(back.shape, BF),
                vm(sel.shape, BF),
                vm(rowsel.shape, BF),
                vm(colsel.shape, BF),
                vm((6, ROWS, D1), BF),
                vm((6, ROWS, 128), BF),
                vm((6, ROWS, D1), BF),
                vm((6, ROWS, D1), BF),
                vm((4, 304, D1), BF),
                vm((3, 64, 384), F32),
                vm((4, 4, 304, 128), BF),
                vm((4, 4, 72, D1), BF),
                vm((16, 288, 128), F32),
                vm((8, 2, 256, D2), BF),
                vm((8, 288, 128), BF),
                vm((288, D2), BF),
                dma((15,)),
                dma((8,)),
                dma((8,)),
                dma((14,)),
                dma((14,)),
                dma((30,)),
                dma((30,)),
                dma((2,)),
            ],
            compiler_params=pltpu.CompilerParams(
                collective_id=0, has_side_effects=True, vmem_limit_bytes=60 * 1024 * 1024
            ),
            cost_estimate=pl.CostEstimate(flops=10**10, bytes_accessed=2 * 10**7, transcendentals=4 * 10**6),
        )(
            tokens.reshape(4, 4, 72, D1), region_labels.transpose(1, 0, 2), fine_qkv, fine_proj, merge_weight, merged_qkv.T, merged_proj,
            order, back, sel, rowsel, colsel,
        )
        return fine_out.reshape(4, 12, 24, D1), merged_out.reshape(6, 12, 4, D2).transpose(2, 0, 1, 3)

    in_specs = (
        P(None, "lat", "lon", None),
        P(None, "lat", "lon"),
        P(),
        P(),
        P(),
        P(None, "lat"),
        P("lat", None),
    )
    out_specs = (P(None, "lat", "lon", None), P(None, "lat", "lon", None))
    return jax.shard_map(shards, mesh=mesh, in_specs=in_specs, out_specs=out_specs, check_vma=False)
```
